512 devices in a mesh: pipe: 16 (over z_hi, x), ctx: 32 (over y, z_lo, core).
Axes of the slice: x: 4, y: 8, z: 8 (z_hi: 4, z_lo: 2; z = z_hi * 2 + z_lo), core: 2. Of those that a mesh axis runs over, the one named last changes fastest.
Arguments:
- queries: bfloat16 [16, 4096, 4096], P('pipe', 'ctx'), may hold values from -32 to 32
- keys: bfloat16 [16, 4096, 512], P('pipe', 'ctx'), may hold values from -32 to 32
- values: bfloat16 [16, 4096, 512], P('pipe', 'ctx'), may hold values from -6 to 6
- out_grad: bfloat16 [16, 4096, 4096], P('pipe', 'ctx'), may hold values from -6 to 6
- doc_ids: int32 [16, 4096], P('pipe', 'ctx'), may hold values from 0 to 15, never falling along the last dimension, each value on 1 to 512 neighbouring positions
Outputs:
- received_acts: bfloat16 [16, 4096, 4096], P('pipe', 'ctx')
- received_dq: bfloat16 [16, 4096, 4096], P('pipe', 'ctx')
- key_grads: bfloat16 [16, 4096, 512], P('pipe', 'ctx')
- value_grads: bfloat16 [16, 4096, 512], P('pipe', 'ctx')
The draws below stay inside these ranges and needn't reach their ends.
Inputs may be any that keep to these rules, and one draw needn't show every extreme that they name: `doc_ids`: along each section's sequence the ids never fall; every id from 0 to 15 names one run of 1 to 512 consecutive tokens, and some run has exactly 512 tokens.
All inputs are finite; a program needn't handle non-finite values.
Results may differ from the reference program's by a relative error of at most 0.039.
The reference program's roundings to bfloat16 on the way (of `weights_b`, `attended`, `grad_scores` and `grad_q`) count: a program that leaves them out, or rounds other values in their place, can miss the bound.
Values may be sent and summed in bfloat16 or wider, within the bound.
No kernel may reach another device: no remote copies, remote signals or barrier semaphores. Data moves between devices by JAX's collectives and lax.ppermute only.
A program may use at most 128 MiB of HBM per device.

```python
import math
import jax
import jax.numpy as jnp
import numpy as np
from jax import lax

HQ = 32
HK = 4
DH = 128
TOK_DEV = 128
REACH = 4
SECTIONS = 16
SEQ = 4096
GROUP = 8
DOC_MOST = 512
DOCS = 16
N_CTX = 32


def draw_queries(key, part):
    key = jax.random.fold_in(key, 1)
    jitter = jax.random.normal(key, (SECTIONS, SEQ, HK, GROUP, DH), jnp.float32)
    return jitter.reshape(SECTIONS, SEQ, HQ * DH).astype(jnp.bfloat16)


def draw_keys(key, part):
    key = jax.random.fold_in(key, 3)
    jitter = jax.random.normal(key, (SECTIONS, SEQ, HK, DH), jnp.float32)
    return jitter.reshape(SECTIONS, SEQ, HK * DH).astype(jnp.bfloat16)


def level_of(key, dims, cuts, least, top_value):
    factor_of = 1.0
    for dim, shards_of in cuts:
        heights = jax.random.uniform(jax.random.fold_in(jax.random.fold_in(key, 6), dim), (shards_of,), jnp.float32, least / len(cuts), top_value / len(cuts))
        factor_of = factor_of * jnp.repeat(jnp.exp(heights), dims[dim] // shards_of).reshape((-1,) + (1,) * (len(dims) - 1 - dim))
    return factor_of


def split_up(number_of, total, limit, skew):
    portions = [(1 << 20) // math.isqrt(standing ** skew) + 1 for standing in range(2, number_of + 1)]
    rest, given = total - limit - (number_of - 1), [1] * (number_of - 1)
    while rest > 0:
        free = [i for i in range(number_of - 1) if given[i] < limit]
        mass, remaining = sum([portions[i] for i in free]), rest
        for i in free:
            addition = min(limit - given[i], max(1, remaining * portions[i] // mass), rest)
            given[i] = given[i] + addition
            rest = rest - addition
    return np.array([limit] + given)


def ragged(rng, amount, total, most, lean):
    if amount == 2:
        one = jax.random.randint(rng, (), max(1, total - most), min(most, total - 1) + 1)
        return jnp.stack([one, total - one])
    lengths = jnp.asarray(split_up(amount, total, most, lean), jnp.int32)
    pairs = (amount - 1) // 2
    donor, sink = lengths[1:1 + 2 * pairs:2], lengths[2:2 + 2 * pairs:2]
    slack = jnp.minimum(donor - 1, most - sink)
    moved = jax.random.randint(jax.random.fold_in(rng, 1), (pairs,), 0, 1 << 20) % (slack + 1)
    lengths = lengths.at[1:1 + 2 * pairs:2].set(donor - moved).at[2:2 + 2 * pairs:2].set(sink + moved)
    return lengths[jax.random.permutation(jax.random.fold_in(rng, 2), amount)]


def noise(own_key, extent, scale, bound, split=(), kind=jnp.bfloat16):
    level = level_of(own_key, extent, split, -0.22, 0.18) if split else 1.0
    result = jax.random.normal(own_key, extent, jnp.float32) * scale * level
    return jnp.minimum(jnp.maximum(result, -bound), bound).astype(kind)


def setup_inputs(seed: int = 0) -> dict:
    splits = jax.random.split(jax.random.key(seed), 6)
    return {
        "queries": draw_queries(jax.random.fold_in(splits[5], 71), 0),
        "keys": draw_keys(jax.random.fold_in(splits[5], 71), 0),
        "values": noise(splits[2], (SECTIONS, SEQ, HK * DH), 1.0, 6.0, ((0, 16), (1, 32))),
        "out_grad": noise(splits[3], (SECTIONS, SEQ, HQ * DH), 1.0, 6.0, ((0, 16), (1, 32))),
        "doc_ids": jax.vmap(lambda own: jnp.searchsorted(jnp.cumsum(ragged(own, DOCS, SEQ, DOC_MOST, 2)), jnp.arange(SEQ), side="right"))(jax.random.split(splits[4], SECTIONS)).reshape((SECTIONS, SEQ)).astype(jnp.int32),
    }


def rounded(array):
    return lax.optimization_barrier(array.astype(jnp.bfloat16)).astype(jnp.float32)


def window_grads(q_rows, k_win, v_win, d_rows, q_mark, k_mark, q_pos, k_pos):
    row_count = q_rows.shape[0]
    key_count = k_win.shape[0]
    q_heads = q_rows.astype(jnp.float32).reshape(row_count, HK, GROUP, DH)
    k_heads = k_win.astype(jnp.float32).reshape(key_count, HK, DH)
    v_heads = v_win.astype(jnp.float32).reshape(key_count, HK, DH)
    d_heads = d_rows.astype(jnp.float32).reshape(row_count, HK, GROUP, DH)
    scaling = DH ** -0.5
    visible = (q_mark[:, None] == k_mark[None, :]) & (k_pos[None, :] <= q_pos[:, None])
    scores = jnp.einsum("tagd,uad->agtu", q_heads, k_heads) * scaling
    scores = jnp.where(visible, scores, -1e30)
    row_max = jnp.max(scores, axis=-1, keepdims=True)
    raised = jnp.where(visible, jnp.exp(scores - row_max), 0.0)
    weights = raised / jnp.sum(raised, axis=-1, keepdims=True)
    weights_b = rounded(weights)
    attended = rounded(jnp.einsum("agtu,uad->tagd", weights_b, v_heads))
    grad_weights = jnp.einsum("tagd,uad->agtu", d_heads, v_heads)
    row_delta = jnp.einsum("tagd,tagd->agt", d_heads, attended)
    grad_scores = rounded(weights * (grad_weights - row_delta[..., None]))
    grad_q = jnp.einsum("agtu,uad->tagd", grad_scores, k_heads) * scaling
    grad_k = jnp.einsum("agtu,tagd->uad", grad_scores, q_heads) * scaling
    grad_v = jnp.einsum("agtu,tagd->uad", weights_b, d_heads)
    return (attended.reshape(row_count, HQ * DH), grad_q.reshape(row_count, HQ * DH),
            grad_k.reshape(key_count, HK * DH), grad_v.reshape(key_count, HK * DH))


def section_pass(section_q, section_k, section_v, section_d, section_docs):
    doc_marks = section_docs + 1
    pad_rows = REACH * TOK_DEV
    key_count = pad_rows + TOK_DEV
    k_pad = jnp.concatenate([jnp.zeros((pad_rows, HK * DH), section_k.dtype), section_k], axis=0)
    v_pad = jnp.concatenate([jnp.zeros((pad_rows, HK * DH), section_v.dtype), section_v], axis=0)
    m_pad = jnp.concatenate([jnp.zeros((pad_rows,), jnp.int32), doc_marks.astype(jnp.int32)], axis=0)

    def block_step(accums, block_index):
        acc_k, acc_v = accums
        start = (block_index * TOK_DEV).astype(jnp.int32)
        q_rows = lax.dynamic_slice_in_dim(section_q, start, TOK_DEV, 0)
        d_rows = lax.dynamic_slice_in_dim(section_d, start, TOK_DEV, 0)
        q_mark = lax.dynamic_slice_in_dim(doc_marks, start, TOK_DEV, 0)
        k_win = lax.dynamic_slice_in_dim(k_pad, start, key_count, 0)
        v_win = lax.dynamic_slice_in_dim(v_pad, start, key_count, 0)
        k_mark = lax.dynamic_slice_in_dim(m_pad, start, key_count, 0)
        q_pos = start + jnp.arange(TOK_DEV, dtype=jnp.int32)
        k_pos = start - pad_rows + jnp.arange(key_count, dtype=jnp.int32)
        attended, grad_q, grad_k, grad_v = window_grads(q_rows, k_win, v_win, d_rows, q_mark, k_mark, q_pos, k_pos)
        acc_k = lax.dynamic_update_slice_in_dim(acc_k, lax.dynamic_slice_in_dim(acc_k, start, key_count, 0) + grad_k, start, 0)
        acc_v = lax.dynamic_update_slice_in_dim(acc_v, lax.dynamic_slice_in_dim(acc_v, start, key_count, 0) + grad_v, start, 0)
        return (acc_k, acc_v), (attended, grad_q)

    empty = jnp.zeros((SEQ + pad_rows, HK * DH), jnp.float32)
    (acc_k, acc_v), (attended, grad_q) = lax.scan(block_step, (empty, empty), jnp.arange(N_CTX, dtype=jnp.int32))
    return (attended.reshape(SEQ, HQ * DH).astype(jnp.bfloat16), grad_q.reshape(SEQ, HQ * DH).astype(jnp.bfloat16),
            acc_k[pad_rows:].astype(jnp.bfloat16), acc_v[pad_rows:].astype(jnp.bfloat16))


def reference(queries, keys, values, out_grad, doc_ids):
    def one_section(section_index):
        return section_pass(queries[section_index], keys[section_index], values[section_index],
                          out_grad[section_index], doc_ids[section_index])

    attended, grad_q, grad_k, grad_v = lax.map(one_section, jnp.arange(SECTIONS, dtype=jnp.int32))
    zeros_wide = jnp.zeros((1, SEQ, HQ * DH), jnp.bfloat16)
    received_acts = jnp.concatenate([zeros_wide, attended[:-1]], axis=0)
    received_dq = jnp.concatenate([grad_q[1:], zeros_wide], axis=0)
    return received_acts, received_dq, grad_k, grad_v
```

```python
import jax
import jax.numpy as jnp
from jax import lax
from jax.experimental import pallas as pl
from jax.experimental.pallas import tpu as pltpu
from jax.sharding import PartitionSpec as P

HK = 4
DH = 128
GROUP = 8
ROWS = 128
PAIR = 2
MARK_ROWS = 16
SCALING = DH ** (-0.5)
LOG2E = 1.4426950408889634
F32 = jnp.float32
BF16 = jnp.bfloat16
NT = (((1,), (1,)), ((), ()))
NN = (((1,), (0,)), ((), ()))


def dot(a, b, dims=NN):
    return lax.dot_general(a, b, dims, preferred_element_type=F32)


def kernel(*refs):
    q_ref, d_ref = refs[:2]
    k_refs, v_refs, m_refs = refs[2:7], refs[7:12], refs[12:17]
    attn_ref, dq_ref = refs[17:19]
    g_refs = refs[19:24]
    bias, s_sc, p_sc, ds_sc = refs[24:28]
    u_pos = lax.broadcasted_iota(jnp.int32, (ROWS, ROWS), 0)
    t_pos = lax.broadcasted_iota(jnp.int32, (ROWS, ROWS), 1)
    tri = u_pos <= t_pos

    @pl.when(pl.program_id(0) == 0)
    def _():
        def col(ref):
            row = ref[0:1, :].astype(F32)
            return jnp.transpose(jnp.broadcast_to(row, (ROWS, ROWS)))

        q_mark = jnp.broadcast_to(m_refs[0][0:1, :].astype(F32), (ROWS, ROWS))
        marks = [jnp.where(tri, col(m_refs[0]), col(m_refs[1]))]
        marks += [col(m) for m in m_refs[2:]]
        for j, k_mark in enumerate(marks):
            bias[j] = jnp.where(k_mark == q_mark, 0.0, -1e30)

    ks = [k[...] for k in k_refs]
    vs = [v[...] for v in v_refs]
    k_t = jnp.concatenate([jnp.transpose(k) for k in ks], axis=1)
    v_t = jnp.concatenate([jnp.transpose(v) for v in vs], axis=1)
    width = PAIR * ROWS
    tri_w = jnp.concatenate([tri] * PAIR, axis=1)
    zero = jnp.zeros((ROWS, width), BF16)

    def merged(blocks):
        return [jnp.where(tri_w, blocks[0], blocks[1])] + list(blocks[2:])

    for unit in range(GROUP // PAIR):
        heads = range(unit * PAIR, (unit + 1) * PAIR)
        cols = slice(unit * width, (unit + 1) * width)
        q_t = jnp.concatenate(
            [jnp.transpose(q_ref[:, h * DH : (h + 1) * DH]) for h in heads], axis=1
        )
        d_t = jnp.concatenate(
            [jnp.transpose(d_ref[:, h * DH : (h + 1) * DH]) for h in heads], axis=1
        )
        scores = merged([dot(k, q_t) for k in ks])
        top = None
        for j, s in enumerate(scores):
            b = bias[j]
            s = s + jnp.concatenate([b] * PAIR, axis=1)
            s_sc[unit, j] = s
            m = jnp.max(s.reshape(ROWS // 8, 8, width), axis=0)
            top = m if top is None else jnp.maximum(top, m)
        top = jnp.max(top, axis=0, keepdims=True)
        total = None
        for j in range(4):
            e = jnp.exp2((s_sc[unit, j] - top) * (SCALING * LOG2E))
            s_sc[unit, j] = e
            part = jnp.sum(e.reshape(ROWS // 8, 8, width), axis=0)
            total = part if total is None else total + part
        inv = 1.0 / jnp.sum(total, axis=0, keepdims=True)
        for j in range(4):
            w = s_sc[unit, j] * inv
            s_sc[unit, j] = w
            wb = w.astype(BF16)
            if j == 0:
                p_sc[0, :, cols] = jnp.where(tri_w, wb, zero)
                p_sc[1, :, cols] = jnp.where(tri_w, zero, wb)
            else:
                p_sc[j + 1, :, cols] = wb
        p_all = p_sc[:, :, cols].reshape(5 * ROWS, width)
        att = dot(v_t, p_all).astype(BF16)
        delta = jnp.sum(d_t.astype(F32) * att.astype(F32), axis=0, keepdims=True)
        for i, h in enumerate(heads):
            attn_ref[:, h * DH : (h + 1) * DH] = jnp.transpose(att[:, i * ROWS : (i + 1) * ROWS])
        grads = merged([dot(v, d_t) for v in vs])
        for j, gw in enumerate(grads):
            ds = (s_sc[unit, j] * (gw - delta)).astype(BF16)
            if j == 0:
                ds_sc[0, :, cols] = jnp.where(tri_w, ds, zero)
                ds_sc[1, :, cols] = jnp.where(tri_w, zero, ds)
            else:
                ds_sc[j + 1, :, cols] = ds
        ds_all = ds_sc[:, :, cols].reshape(5 * ROWS, width)
        dq = (dot(k_t, ds_all) * SCALING).astype(BF16)
        for i, h in enumerate(heads):
            dq_ref[:, h * DH : (h + 1) * DH] = jnp.transpose(dq[:, i * ROWS : (i + 1) * ROWS])
    q_stack = jnp.concatenate([q_ref[:, h * DH : (h + 1) * DH] for h in range(GROUP)], axis=0)
    d_stack = jnp.concatenate([d_ref[:, h * DH : (h + 1) * DH] for h in range(GROUP)], axis=0)
    for j in range(5):
        g_refs[j][0, 0] = dot(ds_sc[j], q_stack) * SCALING
        g_refs[j][1, 0] = dot(p_sc[j], d_stack)


def attend(q_rows, d_rows, blocks, first, count):
    width = GROUP * DH
    wide = pl.BlockSpec((ROWS, width), lambda a: (0, first + a))
    wide_out = pl.BlockSpec((ROWS, width), lambda a: (0, a))
    k_spec = pl.BlockSpec((ROWS, DH), lambda a: (first + a, 0))
    v_spec = pl.BlockSpec((ROWS, DH), lambda a: (HK + first + a, 0))
    m_spec = pl.BlockSpec((MARK_ROWS, DH), lambda a: (2 * HK * ROWS // MARK_ROWS, 0))
    g_spec = pl.BlockSpec((2, 1, ROWS, DH), lambda a: (0, a, 0, 0))
    pairs = ROWS * ROWS * 5 * GROUP * count
    return pl.pallas_call(
        kernel,
        grid=(count,),
        in_specs=[wide] * 2 + [k_spec] * 5 + [v_spec] * 5 + [m_spec] * 5,
        out_specs=[wide_out] * 2 + [g_spec] * 5,
        out_shape=[jax.ShapeDtypeStruct((ROWS, count * width), BF16)] * 2
        + [jax.ShapeDtypeStruct((2, count, ROWS, DH), F32)] * 5,
        scratch_shapes=[
            pltpu.VMEM((4, ROWS, ROWS), F32),
            pltpu.VMEM((GROUP // PAIR, 4, ROWS, PAIR * ROWS), F32),
            pltpu.VMEM((5, ROWS, width), BF16),
            pltpu.VMEM((5, ROWS, width), BF16),
        ],
        compiler_params=pltpu.CompilerParams(vmem_limit_bytes=48 * 1024 * 1024),
        cost_estimate=pl.CostEstimate(
            flops=12 * DH * pairs, bytes_accessed=8 << 20, transcendentals=pairs
        ),
    )(q_rows, d_rows, *blocks, *blocks, *blocks)


REACH = 4
CHIP = 2
GROUP_SHARDS = 4
HALF = 2


def pack_kernel(k_ref, v_ref, m_ref, out_ref):
    for a in range(HK):
        cols = slice(a * DH, (a + 1) * DH)
        out_ref[a * ROWS : (a + 1) * ROWS, :] = k_ref[:, cols]
        out_ref[(HK + a) * ROWS : (HK + a + 1) * ROWS, :] = v_ref[:, cols]
    marks = (m_ref[...] + 1).astype(F32).astype(BF16)
    out_ref[2 * HK * ROWS :, :] = jnp.broadcast_to(marks, (MARK_ROWS, ROWS))


def pack(k_rows, v_rows, marks):
    return pl.pallas_call(
        pack_kernel,
        out_shape=jax.ShapeDtypeStruct((2 * HK * ROWS + MARK_ROWS, DH), BF16),
    )(k_rows, v_rows, marks)


def final_kernel(*refs):
    count = len(refs[:-2]) // 2
    for piece in range(count):
        total = refs[2 * piece][...] + refs[2 * piece + 1][...]
        for i in range(HALF):
            a = piece * HALF + i
            for out, which in ((refs[-2], 0), (refs[-1], 1)):
                out[:, a * DH : (a + 1) * DH] = total[which, i].astype(BF16)


def finish(parts):
    return pl.pallas_call(
        final_kernel,
        out_shape=[jax.ShapeDtypeStruct((ROWS, HK * DH), BF16)] * 2,
    )(*parts)


def swapped(block, bit):
    devices = range(lax.axis_size("ctx"))
    return lax.ppermute(block, "ctx", [(i, i ^ bit) for i in devices])


def passed_along(block, axis, distance):
    devices = range(lax.axis_size(axis))
    return lax.ppermute(block, axis, [(i - distance, i) for i in devices if i - distance in devices])


def body(queries, keys, values, out_grad, doc_ids):
    q_rows, d_rows = queries[0], out_grad[0]
    place = lax.axis_index("ctx") % GROUP_SHARDS
    odd_core = place % CHIP == 1
    second_chip = place >= CHIP
    own = pack(keys[0], values[0], doc_ids)
    back = passed_along(own, "ctx", REACH)
    other_chip = swapped(jnp.where(second_chip, back, own), CHIP)
    near = swapped(jnp.where(odd_core, back, own), 1)
    across = swapped(other_chip, 1)
    blocks = (own, back, other_chip, near, across)
    acts, dqs, parts = [], [], []
    for first in range(0, HK, HALF):
        attended, grad_q, g_own, g_back, g_chip, g_near, g_across = attend(
            q_rows, d_rows, blocks, first, HALF
        )
        acts.append(passed_along(attended, "pipe", 1))
        dqs.append(passed_along(grad_q, "pipe", -1))
        got = swapped(jnp.concatenate([g_near, g_across], axis=0), 1)
        got_near, got_across = got[:2], got[2:]
        got_chip = swapped(g_chip + got_across, CHIP)
        g_back = g_back + jnp.where(odd_core, got_near, 0.0) + jnp.where(second_chip, got_chip, 0.0)
        g_own = g_own + jnp.where(odd_core, 0.0, got_near) + jnp.where(second_chip, 0.0, got_chip)
        got_back = passed_along(g_back, "ctx", -REACH)
        parts += [g_own, got_back]
    key_grads, value_grads = finish(parts)
    acts_in = jnp.concatenate(acts, axis=1)
    dq_in = jnp.concatenate(dqs, axis=1)
    return acts_in[None], dq_in[None], key_grads[None], value_grads[None]


def solution(mesh):
    wide = P("pipe", "ctx", None)
    in_specs = (wide, wide, wide, wide, P("pipe", "ctx"))
    return jax.shard_map(body, mesh=mesh, in_specs=in_specs, out_specs=(wide,) * 4, check_vma=False)
```

```python
import jax
import jax.numpy as jnp
from jax import lax
from jax.experimental import pallas as pl
from jax.experimental.pallas import tpu as pltpu
from jax.sharding import PartitionSpec as P

HK = 4
DH = 128
GROUP = 8
ROWS = 128
PAIR = 8
MARK_ROWS = 16
SCALING = DH ** (-0.5)
TOP_POWER = 14
LOG2E = 1.4426950408889634
F32 = jnp.float32
BF16 = jnp.bfloat16
NT = (((1,), (1,)), ((), ()))
NN = (((1,), (0,)), ((), ()))


def dot(a, b, dims=NN):
    return lax.dot_general(a, b, dims, preferred_element_type=F32)


def kernel(*refs):
    place, q_ref, d_ref = refs[:3]
    k_refs, v_refs, m_refs = refs[3:9], refs[9:15], refs[15:21]
    attn_ref, dq_ref, turn_ref = refs[21:24]
    own_ref, back_ref, chip_ref, sent_ref = refs[24:28]
    bias, s_sc, p_sc, ds_sc = refs[28:32]
    odd_core = place[0] == 1
    turns_attn = place[1] == 1

    def read(block_refs):
        own, back, chip, across, near_own, near_back = [r[...] for r in block_refs]
        return [own, back, chip, across, jnp.where(odd_core, near_own, near_back)]

    u_pos = lax.broadcasted_iota(jnp.int32, (ROWS, ROWS), 0)
    t_pos = lax.broadcasted_iota(jnp.int32, (ROWS, ROWS), 1)
    tri = u_pos <= t_pos

    @pl.when(pl.program_id(0) == 0)
    def _():
        def col(marks):
            return jnp.transpose(jnp.broadcast_to(marks[0:1, :].astype(F32), (ROWS, ROWS)))

        rows = read(m_refs)
        q_mark = jnp.broadcast_to(rows[0][0:1, :].astype(F32), (ROWS, ROWS))
        marks = [jnp.where(tri, col(rows[0]), col(rows[1]))] + [col(m) for m in rows[2:]]
        for j, k_mark in enumerate(marks):
            bias[j] = jnp.where(k_mark == q_mark, 0.0, -1e30)

    ks = read(k_refs)
    vs = read(v_refs)
    k_t = jnp.concatenate([jnp.transpose(k) for k in ks], axis=1)
    v_t = jnp.concatenate([jnp.transpose(v) for v in vs], axis=1)
    width = PAIR * ROWS
    tri_w = jnp.concatenate([tri] * PAIR, axis=1)
    zero = jnp.zeros((ROWS, width), BF16)

    def merged(blocks):
        return [jnp.where(tri_w, blocks[0], blocks[1])] + list(blocks[2:])

    for unit in range(GROUP // PAIR):
        heads = range(unit * PAIR, (unit + 1) * PAIR)
        cols = slice(unit * width, (unit + 1) * width)
        q_u = jnp.concatenate([q_ref[:, h * DH : (h + 1) * DH] for h in heads], axis=0)
        d_u = jnp.concatenate([d_ref[:, h * DH : (h + 1) * DH] for h in heads], axis=0)
        d_t = jnp.concatenate(
            [jnp.transpose(d_ref[:, h * DH : (h + 1) * DH]) for h in heads], axis=1
        )
        scores = merged([dot(k, q_u, NT) for k in ks])
        top = None
        for j, s in enumerate(scores):
            b = bias[j]
            s = s + jnp.concatenate([b] * PAIR, axis=1)
            s_sc[unit, j] = s
            m = jnp.max(s.reshape(ROWS // 8, 8, width), axis=0)
            top = m if top is None else jnp.maximum(top, m)
        top = jnp.max(top, axis=0, keepdims=True)
        total = None
        for j in range(4):
            e = jnp.exp2((s_sc[unit, j] - top) * (SCALING * LOG2E))
            s_sc[unit, j] = e
            part = jnp.sum(e.reshape(ROWS // 8, 8, width), axis=0)
            total = part if total is None else total + part
        inv = 1.0 / jnp.sum(total, axis=0, keepdims=True)
        for j in range(4):
            w = s_sc[unit, j] * inv
            wb = w.astype(BF16)
            if j == 0:
                p_sc[0, :, cols] = jnp.where(tri_w, wb, zero)
                p_sc[1, :, cols] = jnp.where(tri_w, zero, wb)
            else:
                p_sc[j + 1, :, cols] = wb
        p_all = p_sc[:, :, cols].reshape(5 * ROWS, width)
        att = dot(v_t, p_all).astype(BF16)
        delta = jnp.sum(d_t.astype(F32) * att.astype(F32), axis=0, keepdims=True)
        for i, h in enumerate(heads):
            attn_h = jnp.transpose(att[:, i * ROWS : (i + 1) * ROWS])
            attn_ref[:, h * DH : (h + 1) * DH] = attn_h
            turn_ref[:, h * DH : (h + 1) * DH] = attn_h
        grads = merged([dot(v, d_u, NT) for v in vs])
        for j, gw in enumerate(grads):
            ds = (s_sc[unit, j] * inv * (gw - delta)).astype(BF16)
            if j == 0:
                ds_sc[0, :, cols] = jnp.where(tri_w, ds, zero)
                ds_sc[1, :, cols] = jnp.where(tri_w, zero, ds)
            else:
                ds_sc[j + 1, :, cols] = ds
        ds_all = ds_sc[:, :, cols].reshape(5 * ROWS, width)
        dq = (dot(k_t, ds_all) * SCALING).astype(BF16)
        for i, h in enumerate(heads):
            head = slice(h * DH, (h + 1) * DH)
            dq_h = jnp.transpose(dq[:, i * ROWS : (i + 1) * ROWS])
            dq_ref[:, head] = dq_h
            turn_ref[:, head] = jnp.where(turns_attn, turn_ref[:, head], dq_h)
    q_stack = jnp.concatenate([q_ref[:, h * DH : (h + 1) * DH] for h in range(GROUP)], axis=0)
    d_stack = jnp.concatenate([d_ref[:, h * DH : (h + 1) * DH] for h in range(GROUP)], axis=0)
    dk = dot(ds_sc[...].reshape(5 * ROWS, GROUP * ROWS), q_stack) * SCALING
    dv = dot(p_sc[...].reshape(5 * ROWS, GROUP * ROWS), d_stack)
    def blocks_of(grads):
        return [grads[j * ROWS : (j + 1) * ROWS] for j in range(5)]

    for which, grads in enumerate((dk, dv)):
        own, back, chip, across, near = blocks_of(grads)
        own_ref[which, 0] = own
        peak = jnp.max(jnp.max(jnp.abs(grads[ROWS:]), axis=0, keepdims=True), axis=1, keepdims=True)
        power = jnp.ceil(jnp.log2(jnp.maximum(peak, 1e-30))) - TOP_POWER
        scale = jnp.exp2(-power)
        back_ref[which, 0] = back * scale
        chip_ref[which, 0] = chip * scale
        sent_ref[which, 0] = near * scale
        sent_ref[2 + which, 0] = across * scale
        sent_ref[4 + which, 0] = jnp.broadcast_to(power, (ROWS, DH))


def attend(place, q_rows, d_rows, blocks, first, count, weight):
    width = GROUP * DH
    wide = pl.BlockSpec((ROWS, width), lambda a: (0, first + a))
    wide_out = pl.BlockSpec((ROWS, width), lambda a: (0, a))
    k_spec = pl.BlockSpec((ROWS, DH), lambda a: (first + a, 0))
    v_spec = pl.BlockSpec((ROWS, DH), lambda a: (HK + first + a, 0))
    m_spec = pl.BlockSpec((MARK_ROWS, DH), lambda a: (2 * HK * ROWS // MARK_ROWS, 0))
    g_spec = pl.BlockSpec((2, 1, ROWS, DH), lambda a: (0, a, 0, 0))
    sent_spec = pl.BlockSpec((6, 1, ROWS, DH), lambda a: (0, a, 0, 0))
    pairs = ROWS * ROWS * 5 * GROUP * count
    return pl.pallas_call(
        kernel,
        grid=(count,),
        in_specs=[pl.BlockSpec(memory_space=pltpu.SMEM)] + [wide] * 2 + [k_spec] * 6 + [v_spec] * 6 + [m_spec] * 6,
        out_specs=[wide_out] * 3 + [g_spec] * 3 + [sent_spec],
        out_shape=[jax.ShapeDtypeStruct((ROWS, count * width), BF16)] * 3
        + [jax.ShapeDtypeStruct((2, count, ROWS, DH), F32)] * 3
        + [jax.ShapeDtypeStruct((6, count, ROWS, DH), F32)],
        scratch_shapes=[
            pltpu.VMEM((4, ROWS, ROWS), F32),
            pltpu.VMEM((GROUP // PAIR, 4, ROWS, PAIR * ROWS), F32),
            pltpu.VMEM((5, ROWS, width), BF16),
            pltpu.VMEM((5, ROWS, width), BF16),
        ],
        compiler_params=pltpu.CompilerParams(vmem_limit_bytes=60 * 1024 * 1024),
        cost_estimate=pl.CostEstimate(
            flops=weight * 12 * DH * pairs, bytes_accessed=8 << 20, transcendentals=pairs
        ),
    )(place, q_rows, d_rows, *blocks, *blocks, *blocks)


REACH = 4
CHIP = 2
GROUP_SHARDS = 4
HALF = 4
RUN = 4
SENT = jnp.float16
WEIGHT = 20


def pack_kernel(k_ref, v_ref, m_ref, out_ref):
    for a in range(HK):
        cols = slice(a * DH, (a + 1) * DH)
        out_ref[a * ROWS : (a + 1) * ROWS, :] = k_ref[:, cols]
        out_ref[(HK + a) * ROWS : (HK + a + 1) * ROWS, :] = v_ref[:, cols]
    marks = (m_ref[...] + 1).astype(F32).astype(BF16)
    out_ref[2 * HK * ROWS :, :] = jnp.broadcast_to(marks, (MARK_ROWS, ROWS))


def pack(k_rows, v_rows, marks):
    return pl.pallas_call(
        pack_kernel,
        out_shape=jax.ShapeDtypeStruct((2 * HK * ROWS + MARK_ROWS, DH), BF16),
    )(k_rows, v_rows, marks)


def laid(power):
    rows = power[:, :, 0, :].reshape(2 * HK, DH)
    return jnp.pad(rows, ((0, MARK_ROWS - 2 * HK), (0, 0)))


def parcel(values, power):
    return jnp.concatenate([values.reshape(2 * HK * ROWS, DH), laid(power)], axis=0).astype(SENT)


def swapped(block, bit):
    devices = range(lax.axis_size("ctx"))
    return lax.ppermute(block, "ctx", [(i, i ^ bit) for i in devices])


def passed_along(block, axis, distance):
    devices = range(lax.axis_size(axis))
    return lax.ppermute(block, axis, [(i - distance, i) for i in devices if i - distance in devices])


def relays(shard):
    return shard % CHIP == 1


def over_all(block, step):
    sections, shards = lax.axis_size("pipe"), lax.axis_size("ctx")
    route = []
    for s in range(sections):
        to = s + step
        for c in range(shards):
            if 0 <= to < sections and (to // RUN == s // RUN or not relays(c)):
                route.append((s * shards + c, to * shards + c))
    return lax.ppermute(block, ("pipe", "ctx"), route)


def relay(block, legs):
    shards = lax.axis_size("ctx")
    route = [(s * shards + c, t * shards + c) for s, t in legs for c in range(shards) if relays(c)]
    return lax.ppermute(block, ("pipe", "ctx"), route)


def legs_round(sections):
    runs = range(0, sections, RUN)
    last = RUN - 1
    return [(r + last, r) for r in runs[:-1]] + [(r, r + last) for r in runs[1:]]


def legs_over(sections):
    runs = range(0, sections, RUN)
    last = RUN - 1
    return [(r, r + RUN) for r in runs[:-1]] + [(r + last, r + last - RUN) for r in runs[1:]]


def finish_kernel(own_ref, back_ref, chip_ref, k_ref, v_ref):
    size = 2 * HK * ROWS
    for tile in range(2 * HK):
        which, a = tile // HK, tile % HK
        rows = slice(tile * ROWS, (tile + 1) * ROWS)
        total = own_ref[which, a]
        for ref in (back_ref, chip_ref):
            total = total + ref[rows] * jnp.exp2(ref[size + tile : size + tile + 1, :])
        out = (k_ref, v_ref)[which]
        out[:, a * DH : (a + 1) * DH] = total.astype(BF16)


def finish(*parts):
    return pl.pallas_call(
        finish_kernel,
        out_shape=[jax.ShapeDtypeStruct((ROWS, HK * DH), BF16)] * 2,
    )(*parts)


def body(queries, keys, values, out_grad, doc_ids):
    q_rows, d_rows = queries[0], out_grad[0]
    place = lax.axis_index("ctx") % GROUP_SHARDS
    odd_core = place % CHIP == 1
    second_chip = place >= CHIP
    turn = lax.axis_index("pipe") % RUN
    first_in_run, last_in_run = turn == 0, turn == RUN - 1
    own = pack(keys[0], values[0], doc_ids)
    chip = passed_along(own, "ctx", CHIP)
    back = passed_along(own, "ctx", REACH)
    near_own = swapped(own, 1)
    near_back = swapped(back, 1)
    across = swapped(chip, 1)
    blocks = (own, back, chip, across, near_own, near_back)
    flags = jnp.stack([odd_core, last_in_run]).astype(jnp.int32)
    attended, grad_q, turned, g_own, g_back, g_chip, sent = attend(
        flags, q_rows, d_rows, blocks, 0, HK, WEIGHT
    )
    sections = lax.axis_size("pipe")
    turned = relay(turned, legs_round(sections))
    acts_in = over_all(attended, 1)
    dq_in = over_all(grad_q, -1)
    got = swapped(sent.astype(SENT), 1)
    turned, got = lax.optimization_barrier((turned, got))
    power, got_power = sent[4:], got[4:].astype(F32)
    got_near, got_across = got[:2].astype(F32), got[2:4].astype(F32)
    both = jnp.maximum(power, got_power) + 1
    mine = jnp.exp2(power - both)
    theirs = jnp.exp2(got_power - both)
    theirs_back = jnp.where(odd_core, theirs, 0.0)
    theirs_own = jnp.where(odd_core, 0.0, jnp.exp2(got_power))
    for_chip = parcel(g_chip * mine + got_across * theirs, both)
    for_back = parcel(g_back * mine + got_near * theirs_back, both)
    got_chip = passed_along(for_chip, "ctx", -CHIP)
    got_back = passed_along(for_back, "ctx", -REACH)
    turned = relay(turned, legs_over(sections))
    g_own = g_own + got_near * theirs_own
    key_grads, value_grads = finish(g_own, got_back.astype(F32), got_chip.astype(F32))
    acts_in = jnp.where(odd_core & first_in_run, turned, acts_in)
    dq_in = jnp.where(odd_core & last_in_run, turned, dq_in)
    return acts_in[None], dq_in[None], key_grads[None], value_grads[None]


def solution(mesh):
    wide = P("pipe", "ctx", None)
    in_specs = (wide, wide, wide, wide, P("pipe", "ctx"))
    return jax.shard_map(body, mesh=mesh, in_specs=in_specs, out_specs=(wide,) * 4, check_vma=False)
```

```python
import jax
import jax.numpy as jnp
from jax import lax
from jax.experimental import pallas as pl
from jax.experimental.pallas import tpu as pltpu
from jax.sharding import PartitionSpec as P

HK = 4
DH = 128
GROUP = 8
ROWS = 128
PAIR = 8
MARK_ROWS = 16
SCALING = DH ** (-0.5)
TOP_POWER = 14
LOG2E = 1.4426950408889634
F32 = jnp.float32
BF16 = jnp.bfloat16
NT = (((1,), (1,)), ((), ()))
NN = (((1,), (0,)), ((), ()))


def dot(a, b, dims=NN):
    return lax.dot_general(a, b, dims, preferred_element_type=F32)


def kernel(*refs):
    place, q_ref, d_ref = refs[:3]
    k_refs, v_refs, m_refs = refs[3:9], refs[9:15], refs[15:21]
    attn_ref, dq_ref, turn_ref = refs[21:24]
    own_ref, back_ref, chip_ref, sent_ref = refs[24:28]
    bias, s_sc, p_sc, ds_sc = refs[28:32]
    odd_core = place[0] == 1
    turns_attn = place[1] == 1

    def read(block_refs):
        own, back, chip, across, near_own, near_back = [r[...] for r in block_refs]
        return [own, back, chip, across, jnp.where(odd_core, near_own, near_back)]

    u_pos = lax.broadcasted_iota(jnp.int32, (ROWS, ROWS), 0)
    t_pos = lax.broadcasted_iota(jnp.int32, (ROWS, ROWS), 1)
    tri = u_pos <= t_pos

    @pl.when(pl.program_id(0) == 0)
    def _():
        def col(marks):
            return jnp.transpose(jnp.broadcast_to(marks[0:1, :].astype(F32), (ROWS, ROWS)))

        rows = read(m_refs)
        q_mark = jnp.broadcast_to(rows[0][0:1, :].astype(F32), (ROWS, ROWS))
        marks = [jnp.where(tri, col(rows[0]), col(rows[1]))] + [col(m) for m in rows[2:]]
        for j, k_mark in enumerate(marks):
            bias[j] = jnp.where(k_mark == q_mark, 0.0, -1e30)

    ks = read(k_refs)
    vs = read(v_refs)
    k_t = jnp.concatenate([jnp.transpose(k) for k in ks], axis=1)
    v_t = jnp.concatenate([jnp.transpose(v) for v in vs], axis=1)
    width = PAIR * ROWS
    tri_w = jnp.concatenate([tri] * PAIR, axis=1)
    zero = jnp.zeros((ROWS, width), BF16)

    def merged(blocks):
        return [jnp.where(tri_w, blocks[0], blocks[1])] + list(blocks[2:])

    for unit in range(GROUP // PAIR):
        heads = range(unit * PAIR, (unit + 1) * PAIR)
        cols = slice(unit * width, (unit + 1) * width)
        q_u = jnp.concatenate([q_ref[:, h * DH : (h + 1) * DH] for h in heads], axis=0)
        d_u = jnp.concatenate([d_ref[:, h * DH : (h + 1) * DH] for h in heads], axis=0)
        d_t = jnp.concatenate(
            [jnp.transpose(d_ref[:, h * DH : (h + 1) * DH]) for h in heads], axis=1
        )
        scores = merged([dot(k, q_u, NT) for k in ks])
        top = None
        for j, s in enumerate(scores):
            b = bias[j]
            s = s + jnp.concatenate([b] * PAIR, axis=1)
            s_sc[unit, j] = s
            m = jnp.max(s.reshape(ROWS // 8, 8, width), axis=0)
            top = m if top is None else jnp.maximum(top, m)
        top = jnp.max(top, axis=0, keepdims=True)
        total = None
        for j in range(4):
            e = jnp.exp2((s_sc[unit, j] - top) * (SCALING * LOG2E))
            s_sc[unit, j] = e
            part = jnp.sum(e.reshape(ROWS // 8, 8, width), axis=0)
            total = part if total is None else total + part
        inv = 1.0 / jnp.sum(total, axis=0, keepdims=True)
        for j in range(4):
            w = s_sc[unit, j] * inv
            wb = w.astype(BF16)
            if j == 0:
                p_sc[0, :, cols] = jnp.where(tri_w, wb, zero)
                p_sc[1, :, cols] = jnp.where(tri_w, zero, wb)
            else:
                p_sc[j + 1, :, cols] = wb
        p_all = p_sc[:, :, cols].reshape(5 * ROWS, width)
        att = dot(v_t, p_all).astype(BF16)
        delta = jnp.sum(d_t.astype(F32) * att.astype(F32), axis=0, keepdims=True)
        for i, h in enumerate(heads):
            attn_h = jnp.transpose(att[:, i * ROWS : (i + 1) * ROWS])
            attn_ref[:, h * DH : (h + 1) * DH] = attn_h
            turn_ref[:, h * DH : (h + 1) * DH] = attn_h
        grads = merged([dot(v, d_u, NT) for v in vs])
        for j, gw in enumerate(grads):
            ds = (s_sc[unit, j] * inv * (gw - delta)).astype(BF16)
            if j == 0:
                ds_sc[0, :, cols] = jnp.where(tri_w, ds, zero)
                ds_sc[1, :, cols] = jnp.where(tri_w, zero, ds)
            else:
                ds_sc[j + 1, :, cols] = ds
        ds_all = ds_sc[:, :, cols].reshape(5 * ROWS, width)
        dq = (dot(k_t, ds_all) * SCALING).astype(BF16)
        for i, h in enumerate(heads):
            head = slice(h * DH, (h + 1) * DH)
            dq_h = jnp.transpose(dq[:, i * ROWS : (i + 1) * ROWS])
            dq_ref[:, head] = dq_h
            turn_ref[:, head] = jnp.where(turns_attn, turn_ref[:, head], dq_h)
    q_stack = jnp.concatenate([q_ref[:, h * DH : (h + 1) * DH] for h in range(GROUP)], axis=0)
    d_stack = jnp.concatenate([d_ref[:, h * DH : (h + 1) * DH] for h in range(GROUP)], axis=0)
    dk = dot(ds_sc[...].reshape(5 * ROWS, GROUP * ROWS), q_stack) * SCALING
    dv = dot(p_sc[...].reshape(5 * ROWS, GROUP * ROWS), d_stack)
    def blocks_of(grads):
        return [grads[j * ROWS : (j + 1) * ROWS] for j in range(5)]

    for which, grads in enumerate((dk, dv)):
        own, back, chip, across, near = blocks_of(grads)
        own_ref[which, 0] = own
        peak = jnp.max(jnp.max(jnp.abs(grads[ROWS:]), axis=0, keepdims=True), axis=1, keepdims=True)
        power = jnp.ceil(jnp.log2(jnp.maximum(peak, 1e-30))) - TOP_POWER
        scale = jnp.exp2(-power)
        back_ref[which, 0] = back * scale
        chip_ref[which, 0] = chip * scale
        sent_ref[which, 0] = near * scale
        sent_ref[2 + which, 0] = across * scale
        sent_ref[4 + which, 0] = jnp.broadcast_to(power, (ROWS, DH))


def attend(place, q_rows, d_rows, blocks, first, count, weight):
    width = GROUP * DH
    wide = pl.BlockSpec((ROWS, width), lambda a: (0, first + a))
    wide_out = pl.BlockSpec((ROWS, width), lambda a: (0, a))
    k_spec = pl.BlockSpec((ROWS, DH), lambda a: (first + a, 0))
    v_spec = pl.BlockSpec((ROWS, DH), lambda a: (HK + first + a, 0))
    m_spec = pl.BlockSpec((MARK_ROWS, DH), lambda a: (2 * HK * ROWS // MARK_ROWS, 0))
    g_spec = pl.BlockSpec((2, 1, ROWS, DH), lambda a: (0, a, 0, 0))
    sent_spec = pl.BlockSpec((6, 1, ROWS, DH), lambda a: (0, a, 0, 0))
    pairs = ROWS * ROWS * 5 * GROUP * count
    return pl.pallas_call(
        kernel,
        grid=(count,),
        in_specs=[pl.BlockSpec(memory_space=pltpu.SMEM)] + [wide] * 2 + [k_spec] * 6 + [v_spec] * 6 + [m_spec] * 6,
        out_specs=[wide_out] * 3 + [g_spec] * 3 + [sent_spec],
        out_shape=[jax.ShapeDtypeStruct((ROWS, count * width), BF16)] * 3
        + [jax.ShapeDtypeStruct((2, count, ROWS, DH), F32)] * 3
        + [jax.ShapeDtypeStruct((6, count, ROWS, DH), F32)],
        scratch_shapes=[
            pltpu.VMEM((4, ROWS, ROWS), F32),
            pltpu.VMEM((GROUP // PAIR, 4, ROWS, PAIR * ROWS), F32),
            pltpu.VMEM((5, ROWS, width), BF16),
            pltpu.VMEM((5, ROWS, width), BF16),
        ],
        compiler_params=pltpu.CompilerParams(vmem_limit_bytes=60 * 1024 * 1024),
        cost_estimate=pl.CostEstimate(
            flops=weight * 12 * DH * pairs, bytes_accessed=8 << 20, transcendentals=pairs
        ),
    )(place, q_rows, d_rows, *blocks, *blocks, *blocks)


REACH = 4
CHIP = 2
GROUP_SHARDS = 4
HALF = 4
RUN = 4
SENT = jnp.float16
WEIGHT = 20


def pack_kernel(k_ref, v_ref, m_ref, out_ref):
    for a in range(HK):
        cols = slice(a * DH, (a + 1) * DH)
        out_ref[a * ROWS : (a + 1) * ROWS, :] = k_ref[:, cols]
        out_ref[(HK + a) * ROWS : (HK + a + 1) * ROWS, :] = v_ref[:, cols]
    marks = (m_ref[...] + 1).astype(F32).astype(BF16)
    out_ref[2 * HK * ROWS :, :] = jnp.broadcast_to(marks, (MARK_ROWS, ROWS))


def pack(k_rows, v_rows, marks):
    return pl.pallas_call(
        pack_kernel,
        out_shape=jax.ShapeDtypeStruct((2 * HK * ROWS + MARK_ROWS, DH), BF16),
    )(k_rows, v_rows, marks)


def laid(power):
    rows = power[:, :, 0, :].reshape(2 * HK, DH)
    return jnp.pad(rows, ((0, MARK_ROWS - 2 * HK), (0, 0)))


def parcel(values, power):
    return jnp.concatenate([values.reshape(2 * HK * ROWS, DH), laid(power)], axis=0).astype(SENT)


def swapped(block, bit):
    devices = range(lax.axis_size("ctx"))
    return lax.ppermute(block, "ctx", [(i, i ^ bit) for i in devices])


def passed_along(block, axis, distance):
    devices = range(lax.axis_size(axis))
    return lax.ppermute(block, axis, [(i - distance, i) for i in devices if i - distance in devices])


def relays(shard):
    return shard % GROUP_SHARDS == 1


def over_all(block, step):
    sections, shards = lax.axis_size("pipe"), lax.axis_size("ctx")
    route = []
    for s in range(sections):
        to = s + step
        for c in range(shards):
            if 0 <= to < sections and (to // RUN == s // RUN or not relays(c)):
                route.append((s * shards + c, to * shards + c))
    return lax.ppermute(block, ("pipe", "ctx"), route)


def relay(block, legs):
    shards = lax.axis_size("ctx")
    route = [(s * shards + c, t * shards + c) for s, t in legs for c in range(shards) if relays(c)]
    return lax.ppermute(block, ("pipe", "ctx"), route)


def legs_round(sections):
    runs = range(0, sections, RUN)
    last = RUN - 1
    return [(r + last, r) for r in runs[:-1]] + [(r, r + last) for r in runs[1:]]


def legs_over(sections):
    runs = range(0, sections, RUN)
    last = RUN - 1
    return [(r, r + RUN) for r in runs[:-1]] + [(r + last, r + last - RUN) for r in runs[1:]]


def finish_kernel(own_ref, back_ref, chip_ref, k_ref, v_ref):
    size = 2 * HK * ROWS
    for tile in range(2 * HK):
        which, a = tile // HK, tile % HK
        rows = slice(tile * ROWS, (tile + 1) * ROWS)
        total = own_ref[which, a]
        for ref in (back_ref, chip_ref):
            total = total + ref[rows] * jnp.exp2(ref[size + tile : size + tile + 1, :])
        out = (k_ref, v_ref)[which]
        out[:, a * DH : (a + 1) * DH] = total.astype(BF16)


def finish(*parts):
    return pl.pallas_call(
        finish_kernel,
        out_shape=[jax.ShapeDtypeStruct((ROWS, HK * DH), BF16)] * 2,
    )(*parts)


def body(queries, keys, values, out_grad, doc_ids):
    q_rows, d_rows = queries[0], out_grad[0]
    place = lax.axis_index("ctx") % GROUP_SHARDS
    odd_core = place % CHIP == 1
    second_chip = place >= CHIP
    turn = lax.axis_index("pipe") % RUN
    first_in_run, last_in_run = turn == 0, turn == RUN - 1
    own = pack(keys[0], values[0], doc_ids)
    chip = passed_along(own, "ctx", CHIP)
    back = passed_along(own, "ctx", REACH)
    near_own = swapped(own, 1)
    near_back = swapped(back, 1)
    across = swapped(chip, 1)
    blocks = (own, back, chip, across, near_own, near_back)
    flags = jnp.stack([odd_core, last_in_run]).astype(jnp.int32)
    attended, grad_q, turned, g_own, g_back, g_chip, sent = attend(
        flags, q_rows, d_rows, blocks, 0, HK, WEIGHT
    )
    sections = lax.axis_size("pipe")
    turned = relay(turned, legs_round(sections))
    acts_in = over_all(attended, 1)
    dq_in = over_all(grad_q, -1)
    got = swapped(sent.astype(SENT), 1)
    turned, got = lax.optimization_barrier((turned, got))
    power, got_power = sent[4:], got[4:].astype(F32)
    got_near, got_across = got[:2].astype(F32), got[2:4].astype(F32)
    both = jnp.maximum(power, got_power) + 1
    mine = jnp.exp2(power - both)
    theirs = jnp.exp2(got_power - both)
    theirs_back = jnp.where(odd_core, theirs, 0.0)
    theirs_own = jnp.where(odd_core, 0.0, jnp.exp2(got_power))
    for_chip = parcel(g_chip * mine + got_across * theirs, both)
    for_back = parcel(g_back * mine + got_near * theirs_back, both)
    got_chip = passed_along(for_chip, "ctx", -CHIP)
    got_back = passed_along(for_back, "ctx", -REACH)
    turned = relay(turned, legs_over(sections))
    g_own = g_own + got_near * theirs_own
    key_grads, value_grads = finish(g_own, got_back.astype(F32), got_chip.astype(F32))
    acts_in = jnp.where(relays(place) & first_in_run, turned, acts_in)
    dq_in = jnp.where(relays(place) & last_in_run, turned, dq_in)
    return acts_in[None], dq_in[None], key_grads[None], value_grads[None]


def solution(mesh):
    wide = P("pipe", "ctx", None)
    in_specs = (wide, wide, wide, wide, P("pipe", "ctx"))
    return jax.shard_map(body, mesh=mesh, in_specs=in_specs, out_specs=(wide,) * 4, check_vma=False)
```
